512 devices in a mesh: gy: 32 (over z_lo, y, core), gz: 16 (over z_hi, x).
Axes of the slice: x: 4, y: 8, z: 8 (z_hi: 4, z_lo: 2; z = z_hi * 2 + z_lo), core: 2. Of those that a mesh axis runs over, the one named last changes fastest.
Arguments:
- coarse: float32 [8, 1, 1024, 1024], P(None, None, 'gy', 'gz'), may hold values from 0 to 1
- labels: int32 [2, 2048, 2048], P(None, 'gy', 'gz'), may hold values from 0 to 7
- mobility: float32 [8], replicated, may hold values from 0.5 to 2
Outputs:
- phase_field: float32 [8, 2, 2048, 2048], P(None, None, 'gy', 'gz')
The draws below stay inside these ranges and needn't reach their ends.
All inputs are finite; a program needn't handle non-finite values.
Results may differ from the reference program's by a relative error of at most 0.0001.
Values sent between devices are 32-bit elements; how exact they have to be, the bound alone decides.
No kernel may reach another device: no remote copies, remote signals or barrier semaphores. Data moves between devices by JAX's collectives and lax.ppermute only.
A program may use at most 64 MiB of HBM per device.

```python
import math
import jax
import jax.numpy as jnp
from jax import lax

P_SIZE = 8
CX = 1
ITERS = 2
FX = 2
CNY = 1024
CNZ = 1024
NY = 2048
NZ = 2048


def with_ends(entries, rng, low, largest):
    longest = entries.shape.index(max(entries.shape))
    spots = []
    for shift in (0, 1):
        where = [jax.random.randint(jax.random.fold_in(rng, axis), (), 0, length) for axis, length in enumerate(entries.shape)]
        where[longest] = (where[longest] + shift) % entries.shape[longest]
        spots.append(tuple(where))
    return entries.at[spots[0]].set(low).at[spots[1]].set(largest)


def block_scale(stream_key, dims, shards, least, largest):
    def one(position, parts):
        draws = jax.random.uniform(jax.random.fold_in(jax.random.fold_in(stream_key, 6), position), (parts,), jnp.float32, least / len(shards), largest / len(shards))
        return jnp.repeat(jnp.exp(draws), dims[position] // parts).reshape((-1,) + (1,) * (len(dims) - position - 1))

    gain = one(*shards[0])
    for cut in shards[1:]:
        gain = gain * one(*cut)
    return gain


def setup_inputs(seed: int = 0) -> dict:
    key_of = jax.random.split(jax.random.key(seed), 4)
    return {
        "coarse": jnp.clip(1.0 * jax.random.uniform(key_of[0], (P_SIZE, CX, CNY, CNZ), jnp.float32) ** block_scale(key_of[0], (P_SIZE, CX, CNY, CNZ), ((2, 32), (3, 16)), -0.2, 0.2), 0.0, 1.0),
        "labels": with_ends(jax.random.randint(key_of[1], (FX, NY, NZ), 0, P_SIZE), jax.random.fold_in(key_of[1], 1), 0, P_SIZE - 1).astype(jnp.int32),
        "mobility": jnp.clip(jnp.exp(jax.random.uniform(key_of[2], (P_SIZE,), jnp.float32, math.log(0.5), math.log(2.0))), 0.5, 2.0),
    }


STEP = 0.075
GAMMA = 0.5
PIN = 1.0


def refine(field, axis):
    count = field.shape[axis]
    lower = lax.slice_in_dim(field, 0, count - 1, axis=axis)
    upper = lax.slice_in_dim(field, 1, count, axis=axis)
    odd_cells = 0.75 * lower + 0.25 * upper
    even_cells = 0.75 * upper + 0.25 * lower
    paired = jnp.stack([odd_cells, even_cells], axis=axis + 1)
    shape = list(field.shape)
    shape[axis] = 2 * (count - 1)
    return paired.reshape(shape)


def advance(padded, labels, mobility):
    center = padded[:, :, 1:-1, 1:-1]
    lap = jnp.roll(center, 1, 1) + jnp.roll(center, -1, 1)
    lap = lap + padded[:, :, 2:, 1:-1] + padded[:, :, :-2, 1:-1]
    lap = lap + padded[:, :, 1:-1, 2:] + padded[:, :, 1:-1, :-2] - 6.0 * center
    phases = jnp.arange(center.shape[0], dtype=jnp.int32)
    onehot = (labels[None] == phases[:, None, None, None]).astype(jnp.float32)
    squared = center * center
    squares = jnp.sum(squared, axis=0, keepdims=True)
    drive = center * (1.0 - squared) - 2.0 * GAMMA * center * (squares - squared) + PIN * (onehot - center)
    return center + STEP * mobility[:, None, None, None] * (lap + drive)


def reference(coarse, labels, mobility):
    padded = jnp.pad(coarse, ((0, 0), (1, 1), (1, 1), (1, 1)), mode="wrap")
    fine = refine(refine(refine(padded, 1), 2), 3)
    phase = fine[:, 1:-1, 1:-1, 1:-1]
    for step in range(ITERS):
        wrapped = jnp.pad(phase, ((0, 0), (0, 0), (1, 1), (1, 1)), mode="wrap")
        phase = advance(wrapped, labels, mobility)
    return phase
```

```python
import jax
import jax.numpy as jnp
from jax import lax
from jax.experimental import pallas as pl
from jax.experimental.pallas import tpu as pltpu
from jax.sharding import PartitionSpec as P

STEP = 0.075
NP = 8
CR, CC = 32, 64
FR, FC = 64, 128
YROWS = 48
ZROWS = 48
F32 = jnp.float32


def lanes(rows):
    return lax.broadcasted_iota(jnp.int32, (rows, 128), 1)


def pack_kernel(coarse, labels, strip, cols):
    lane = lanes(CR)
    packed = jnp.zeros((CR, 128), F32)
    for p in range(NP):
        own = coarse[p]
        both = jnp.concatenate([own, own], axis=1)
        packed = jnp.where(lane // 4 == p, pltpu.roll(both, (4 * p - 62) % 128, 1), packed)
        strip[4 * p : 4 * p + 2, :] = both[30:32]
        strip[4 * p + 2 : 4 * p + 4, :] = both[0:2]
    for x in range(2):
        marks = labels[x].astype(F32)
        spot = 32 + 4 * x
        packed = jnp.where(lane // 2 == spot // 2, pltpu.roll(marks[:CR], spot + 1, 1), packed)
        packed = jnp.where(lane // 2 == spot // 2 + 1, pltpu.roll(marks[CR:], spot + 3, 1), packed)
        strip[32 + 2 * x : 33 + 2 * x, :] = marks[FR - 1 : FR]
        strip[33 + 2 * x : 34 + 2 * x, :] = marks[0:1]
    cols[...] = packed
    strip[36:40, :] = jnp.zeros((4, 128), F32)
    strip[40:42, :] = packed[30:32]
    strip[42:44, :] = packed[0:2]
    strip[44:48, :] = jnp.zeros((4, 128), F32)


def z_weights():
    k = lax.broadcasted_iota(jnp.int32, (256, 256), 0) % 128
    n = lax.broadcasted_iota(jnp.int32, (256, 256), 1)
    z = jnp.where(n < 128, n, jnp.where(n == 128, -1, jnp.where(n == 255, 128, jnp.where(n == 254, -2, jnp.where(n == 253, 129, 999)))))
    column = jnp.where(k < 64, k, jnp.where(k < 66, k - 66, jnp.where(k < 68, k - 2, -999)))
    near = z >> 1
    far = near + 2 * (z & 1) - 1
    return (0.75 * (column == near).astype(F32) + 0.25 * (column == far).astype(F32)).astype(jnp.bfloat16)


def relax_kernel(mobility, coarse, labels, ya, yb, za, zb, out, pad, zm, ze, fm, fe, lm, le, pm, pe):
    y_even = lax.axis_index("gy") % 2 == 0
    z_even = lax.axis_index("gz") % 2 == 0
    high = jnp.where(y_even, ya[1], yb[...])
    low = jnp.where(y_even, yb[...], ya[0])
    left = jnp.where(z_even, zb[0], za[...])
    right = jnp.where(z_even, za[...], zb[1])

    lane = lanes(ZROWS)
    halo = jnp.where(lane % 4 < 2, left, right)
    corner_high = jnp.where(y_even, halo[36:40], halo[40:44])
    corner_low = jnp.where(y_even, halo[40:44], halo[32:36])
    for p in range(NP):
        turn = (64 - 4 * p) % 128
        pad[p, 8 : 8 + CR, :] = pltpu.roll(halo[:CR], turn, 1)
        pad[p, 8 : 8 + CR, 0:CC] = coarse[p]
        inner = lane[0:2] < CC
        pad[p, 6:8, :] = jnp.where(inner, low[4 * p : 4 * p + 2], pltpu.roll(corner_low, turn, 1)[0:2])
        pad[p, 40:42, :] = jnp.where(inner, high[4 * p + 2 : 4 * p + 4], pltpu.roll(corner_high, turn, 1)[2:4])

    cells = pad[...].reshape(NP * 48, 128)
    first = cells.astype(jnp.bfloat16)
    second = (cells - first.astype(F32)).astype(jnp.bfloat16)
    fine = jnp.dot(jnp.concatenate([first, second], axis=1), z_weights(), preferred_element_type=F32)
    zm[...] = fine[:, :128].reshape(NP, 48, 128)
    ze[...] = fine[:, 128:].reshape(NP, 48, 128)
    for p in range(NP):
        for src, dst in ((zm, fm), (ze, fe)):
            mid = 0.75 * src[p, 7:41, :]
            dst[p, pl.ds(6, 34, stride=2), :] = mid + 0.25 * src[p, 6:40, :]
            dst[p, pl.ds(7, 34, stride=2), :] = mid + 0.25 * src[p, 8:42, :]

    marks = jnp.where(lane[:CR] % 2 == 0, pltpu.roll(right[:CR], 127, 1), pltpu.roll(left[:CR], 1, 1))
    for x in range(2):
        lm[x, 8 : 8 + FR, :] = labels[x].astype(F32)
        lm[x, 7:8, :] = low[32 + 2 * x : 33 + 2 * x]
        lm[x, 72:73, :] = high[33 + 2 * x : 34 + 2 * x]
        le[x, 8 : 8 + CR, :] = pltpu.roll(marks, 95 - 4 * x, 1)
        le[x, 8 + CR : 8 + FR, :] = pltpu.roll(marks, 93 - 4 * x, 1)

    rate = [STEP * mobility[p] for p in range(NP)]
    lane8 = lanes(8)
    first_lane, last_lane = lane8 == 0, lane8 == 127

    for t in range(9):
        here = pl.ds(7 + 8 * t, 8)
        above, below = pl.ds(6 + 8 * t, 8), pl.ds(8 + 8 * t, 8)
        ms = [fm[p, here, :] for p in range(NP)]
        es = [fe[p, here, :] for p in range(NP)]
        sm = 4.0 + sum(m * m for m in ms)
        se = 4.0 + sum(e * e for e in es)
        marks_m = [lm[x, here, :] for x in range(2)]
        marks_e = [le[x, here, :] for x in range(2)]
        for p in range(NP):
            m, e = ms[p], es[p]
            west = jnp.where(first_lane, e, pltpu.roll(m, 1, 1))
            east = jnp.where(last_lane, e, pltpu.roll(m, 127, 1))
            lap = (fm[p, above, :] + fm[p, below, :]) + (west + east)
            base = m + rate[p] * (lap - sm * m)
            lap_e = (fe[p, above, :] + fe[p, below, :]) + (m + pltpu.roll(e, 2, 1))
            base_e = e + rate[p] * (lap_e - se * e)
            for x in range(2):
                pm[x, p, here, :] = jnp.where(marks_m[x] == p, base + rate[p], base)
                pe[x, p, here, :] = jnp.where(marks_e[x] == p, base_e + rate[p], base_e)

    for t in range(8):
        here = pl.ds(8 + 8 * t, 8)
        above, below = pl.ds(7 + 8 * t, 8), pl.ds(9 + 8 * t, 8)
        for x in range(2):
            ms = [pm[x, p, here, :] for p in range(NP)]
            sm = 6.0 + sum(m * m for m in ms)
            marks_m = lm[x, here, :]
            for p in range(NP):
                m, e, other = ms[p], pe[x, p, here, :], pm[1 - x, p, here, :]
                west = jnp.where(first_lane, e, pltpu.roll(m, 1, 1))
                east = jnp.where(last_lane, e, pltpu.roll(m, 127, 1))
                lap = (pm[x, p, above, :] + pm[x, p, below, :]) + (west + east) + (other + other)
                change = lap - sm * m
                change = jnp.where(marks_m == p, change + 1.0, change)
                out[p, x, 8 * t : 8 * t + 8, :] = m + rate[p] * change


def swapped(cells, axis, odd):
    count = lax.axis_size(axis)
    pairs = []
    for i in range(odd, count, 2):
        j = (i + 1) % count
        pairs += [(i, j), (j, i)]
    return lax.ppermute(cells, axis, pairs)


def paired(cells, axis, odd):
    count = lax.axis_size(axis)
    return lax.all_gather(cells, axis, axis_index_groups=[[i, (i + 1) % count] for i in range(odd, count, 2)])


def shards(coarse, labels, mobility):
    coarse = coarse.reshape(NP, CR, CC)
    vmem = pl.BlockSpec(memory_space=pltpu.VMEM)
    strip, cols = pl.pallas_call(
        pack_kernel,
        out_shape=(jax.ShapeDtypeStruct((YROWS, 128), F32), jax.ShapeDtypeStruct((CR, 128), F32)),
        in_specs=[vmem, vmem],
        out_specs=(vmem, vmem),
        compiler_params=pltpu.CompilerParams(vmem_limit_bytes=8 << 20),
        cost_estimate=pl.CostEstimate(flops=20000, bytes_accessed=200000, transcendentals=0),
        name="pack",
    )(coarse, labels)
    yb = swapped(strip, "gy", 1)
    ya = paired(strip, "gy", 0)
    sides = jnp.concatenate([cols, ya[0, 40:44], ya[1, 40:44], yb[40:44], jnp.zeros((4, 128), F32)])
    za = swapped(sides, "gz", 0)
    zb = paired(sides, "gz", 1)
    tile = lambda *shape: pltpu.VMEM(shape + (128,), F32)
    out = pl.pallas_call(
        relax_kernel,
        out_shape=jax.ShapeDtypeStruct((NP, 2, FR, FC), F32),
        in_specs=[pl.BlockSpec(memory_space=pltpu.SMEM)] + [vmem] * 6,
        out_specs=vmem,
        scratch_shapes=[
            tile(NP, 48),
            tile(NP, 48),
            tile(NP, 48),
            tile(NP, 88),
            tile(NP, 88),
            tile(2, 80),
            tile(2, 80),
            tile(2, NP, 80),
            tile(2, NP, 80),
        ],
        compiler_params=pltpu.CompilerParams(vmem_limit_bytes=16 << 20),
        cost_estimate=pl.CostEstimate(flops=8000000, bytes_accessed=900000, transcendentals=0),
        name="relax",
    )(mobility, coarse, labels, ya, yb, za, zb)
    return out


def solution(mesh):
    in_specs = (P(None, None, "gy", "gz"), P(None, "gy", "gz"), P())
    out_specs = P(None, None, "gy", "gz")
    return jax.shard_map(shards, mesh=mesh, in_specs=in_specs, out_specs=out_specs, check_vma=False)
```

```python
import jax
import jax.numpy as jnp
from jax import lax
from jax.experimental import pallas as pl
from jax.experimental.pallas import tpu as pltpu
from jax.sharding import PartitionSpec as P

STEP = 0.075
NP = 8
CR, CC = 32, 64
FR, FC = 64, 128
MROWS = 16
F32 = jnp.float32


def lanes(rows):
    return lax.broadcasted_iota(jnp.int32, (rows, 128), 1)


def parities():
    return lax.axis_index("gy") % 2 == 0, lax.axis_index("gz") % 2 == 0


def strips_kernel(coarse_hbm, labels_hbm, mobility_hbm, to_a, to_b, rates, top, bottom, marks, mobility, low, high, sems):
    copies = [
        pltpu.make_async_copy(src, dst, sems.at[i])
        for i, (src, dst) in enumerate(
            (
                (coarse_hbm.at[:, 0:8, :], top),
                (coarse_hbm.at[:, CR - 8 : CR, :], bottom),
                (labels_hbm.at[:, 0:8, :], marks.at[:, 0:8, :]),
                (labels_hbm.at[:, FR - 8 : FR, :], marks.at[:, 8:16, :]),
                (mobility_hbm, mobility),
            )
        )
    ]
    for copy in copies:
        copy.start()
    y_even, _ = parities()
    for copy in copies:
        copy.wait()
    for row, block, strip in ((0, top, low), (6, bottom, high)):
        for p in range(NP):
            strip[p : p + 1, 0:CC] = block[p, row : row + 1, :]
            strip[p : p + 1, CC : 2 * CC] = block[p, row + 1 : row + 2, :]
        for x in range(2):
            strip[8 + x : 9 + x, :] = marks[x, 15 * (row // 6) : 15 * (row // 6) + 1, :].astype(F32)
        strip[10:16, :] = jnp.zeros((6, 128), F32)
    to_a[...] = jnp.where(y_even, high[...], low[...])
    to_b[...] = jnp.where(y_even, low[...], high[...])
    for p in range(NP):
        rates[p : p + 1, :] = jnp.full((1, 128), STEP * mobility[p], F32)


def columns_kernel(coarse, labels, sides):
    lane = lanes(8)
    first, last = jnp.zeros((8, 128), F32), jnp.zeros((8, 128), F32)
    for g in range(4):
        start = 64 * (g // 2) + 2 * (g % 2)
        for p in range(NP):
            own = jnp.concatenate([coarse[p, 8 * g : 8 * g + 8, :], jnp.zeros((8, CC), F32)], axis=1)
            at = start + 4 * p
            first = jnp.where(lane // 2 == at // 2, pltpu.roll(own, at, 1), first)
            last = jnp.where(lane // 2 == at // 2, pltpu.roll(own, (at - 62) % 128, 1), last)
        for k in range(4):
            at = start + 32 + 4 * k
            cells = labels[k % 2, 32 * (k // 2) + 8 * g : 32 * (k // 2) + 8 * g + 8, :].astype(F32)
            first = jnp.where(lane == at, pltpu.roll(cells, at, 1), first)
            last = jnp.where(lane == at, pltpu.roll(cells, at + 1, 1), last)
    sides[0:8, :] = first
    sides[8:16, :] = last


def picked(ya0, ya1, yb):
    y_even, _ = parities()
    return jnp.where(y_even, yb, ya0), jnp.where(y_even, ya1, yb)


def sides_kernel(columns, ya, yb, sides):
    sides[0:16, :] = columns[...]
    lane = lanes(8)
    ends = jnp.zeros((8, 128), F32)
    for j, strip in enumerate(picked(ya[0, 0:8], ya[1, 0:8], yb[0:8])):
        for i in range(2):
            at = 64 + 16 * j + 8 * i
            ends = jnp.where(lane // 2 == at // 2, pltpu.roll(strip, (at - 62 - 64 * i) % 128, 1), ends)
            ends = jnp.where(lane // 2 == at // 2 + 1, pltpu.roll(strip, (at + 2 - 64 * i) % 128, 1), ends)
    sides[16:24, :] = ends


def z_weights():
    k = lax.broadcasted_iota(jnp.int32, (256, 256), 0) % 128
    n = lax.broadcasted_iota(jnp.int32, (256, 256), 1)
    z = jnp.where(n < 128, n, jnp.where(n == 128, -1, jnp.where(n == 255, 128, jnp.where(n == 254, -2, jnp.where(n == 253, 129, 999)))))
    column = jnp.where(k < 64, k, jnp.where(k < 66, k - 66, jnp.where(k < 68, k - 2, -999)))
    near = z >> 1
    far = near + 2 * (z & 1) - 1
    return (0.75 * (column == near).astype(F32) + 0.25 * (column == far).astype(F32)).astype(jnp.bfloat16)


def relax_kernel(rates, coarse, labels, ya, yb, za0, za1, zb, out_hbm, pad, zm, ze, fm, fe, lm, le, pm, pe, out, sems):
    _, z_even = parities()
    low, high = picked(ya[0], ya[1], yb[...])
    za = za0[...] + za1[...]
    left = jnp.where(z_even, zb[0], za)
    right = jnp.where(z_even, za, zb[1])

    lane8 = lanes(8)
    first_lane, last_lane = lane8 == 0, lane8 == 127
    west, east = left[8:16], right[0:8]
    for g in range(4):
        start = 64 * (g // 2) + 2 * (g % 2)
        for p in range(NP):
            at = start + 4 * p
            beside = jnp.where(lane8 < 66, pltpu.roll(west, (64 - at) % 128, 1), pltpu.roll(east, (66 - at) % 128, 1))
            pad[48 * p + 8 + 8 * g : 48 * p + 16 + 8 * g, :] = beside
        for k in range(4):
            rows = slice(8 + 32 * (k // 2) + 8 * g, 16 + 32 * (k // 2) + 8 * g)
            at = start + 32 + 4 * k
            le[k % 2, rows, :] = jnp.where(first_lane, pltpu.roll(west, 128 - at, 1), pltpu.roll(east, 127 - at, 1))
    for p in range(NP):
        pad[48 * p + 8 : 48 * p + 8 + CR, 0:CC] = coarse[p]
    ends = jnp.where(lane8 % 4 < 2, left[16:24], right[16:24])
    for j, strip in enumerate((low, high)):
        for i in range(2):
            beside = pltpu.roll(ends, (-16 * j - 8 * i) % 128, 1)
            cells = pltpu.roll(strip[0:8], CC, 1) if i else strip[0:8]
            pad[pl.ds(6 + 34 * j + i, NP, stride=48), :] = jnp.where(lane8 < CC, cells, beside)

    cells = pad[...]
    first = cells.astype(jnp.bfloat16)
    second = (cells - first.astype(F32)).astype(jnp.bfloat16)
    fine = jnp.dot(jnp.concatenate([first, second], axis=1), z_weights(), preferred_element_type=F32)
    zm[...] = fine[:, :128].reshape(NP, 48, 128)
    ze[...] = fine[:, 128:].reshape(NP, 48, 128)
    for p in range(NP):
        for src, dst in ((zm, fm), (ze, fe)):
            mid = 0.75 * src[p, 7:41, :]
            dst[p, pl.ds(6, 34, stride=2), :] = mid + 0.25 * src[p, 6:40, :]
            dst[p, pl.ds(7, 34, stride=2), :] = mid + 0.25 * src[p, 8:42, :]

    for x in range(2):
        lm[x, 8 : 8 + FR, :] = labels[x].astype(F32)
        lm[x, 7:8, :] = low[8 + x : 9 + x]
        lm[x, 72:73, :] = high[8 + x : 9 + x]

    rate = [rates[p : p + 1, :] for p in range(NP)]

    for t in range(9):
        here = pl.ds(7 + 8 * t, 8)
        above, below = pl.ds(6 + 8 * t, 8), pl.ds(8 + 8 * t, 8)
        ms = [fm[p, here, :] for p in range(NP)]
        es = [fe[p, here, :] for p in range(NP)]
        sm = 4.0 + sum(m * m for m in ms)
        se = 4.0 + sum(e * e for e in es)
        marks_m = [lm[x, here, :] for x in range(2)]
        marks_e = [le[x, here, :] for x in range(2)]
        for p in range(NP):
            m, e = ms[p], es[p]
            west = jnp.where(first_lane, e, pltpu.roll(m, 1, 1))
            east = jnp.where(last_lane, e, pltpu.roll(m, 127, 1))
            lap = (fm[p, above, :] + fm[p, below, :]) + (west + east)
            base = m + rate[p] * (lap - sm * m)
            lap_e = (fe[p, above, :] + fe[p, below, :]) + (m + pltpu.roll(e, 2, 1))
            base_e = e + rate[p] * (lap_e - se * e)
            for x in range(2):
                pm[x, p, here, :] = jnp.where(marks_m[x] == p, base + rate[p], base)
                pe[x, p, here, :] = jnp.where(marks_e[x] == p, base_e + rate[p], base_e)

    copies = []
    for t in range(8):
        here = pl.ds(8 + 8 * t, 8)
        above, below = pl.ds(7 + 8 * t, 8), pl.ds(9 + 8 * t, 8)
        for x in range(2):
            ms = [pm[x, p, here, :] for p in range(NP)]
            sm = 6.0 + sum(m * m for m in ms)
            marks_m = lm[x, here, :]
            for p in range(NP):
                m, e, other = ms[p], pe[x, p, here, :], pm[1 - x, p, here, :]
                west = jnp.where(first_lane, e, pltpu.roll(m, 1, 1))
                east = jnp.where(last_lane, e, pltpu.roll(m, 127, 1))
                lap = (pm[x, p, above, :] + pm[x, p, below, :]) + (west + east) + (other + other)
                change = lap - sm * m
                change = jnp.where(marks_m == p, change + 1.0, change)
                out[p, x, 8 * t : 8 * t + 8, :] = m + rate[p] * change
        if t in (2, 5, 7):
            part = (2, 5, 7).index(t)
            rows = pl.ds(24 * part, 24 if t < 7 else 16)
            copies.append(pltpu.make_async_copy(out.at[:, :, rows, :], out_hbm.at[:, :, rows, :], sems.at[part]))
            copies[-1].start()
    for copy in copies:
        copy.wait()


def exchanged(cells, pairs):
    width = lax.axis_size("gz")
    flat = [(i * width + j, k * width + l) for (i, j), (k, l) in pairs]
    return lax.ppermute(cells, ("gy", "gz"), flat + [(b, a) for a, b in flat])


def paired(cells, axis, odd):
    count = lax.axis_size(axis)
    return lax.all_gather(cells, axis, axis_index_groups=[[i, (i + 1) % count] for i in range(odd, count, 2)])


def shards(coarse, labels, mobility):
    coarse = coarse.reshape(NP, CR, CC)
    vmem = pl.BlockSpec(memory_space=pltpu.VMEM)
    hbm = pl.BlockSpec(memory_space=pltpu.HBM)
    tile = lambda *shape: pltpu.VMEM(shape + (128,), F32)
    to_a, to_b, rates = pl.pallas_call(
        strips_kernel,
        out_shape=(tile(MROWS), tile(MROWS), tile(8)),
        in_specs=[hbm, hbm, hbm],
        out_specs=(vmem,) * 3,
        scratch_shapes=[
            pltpu.VMEM((NP, 8, CC), F32),
            pltpu.VMEM((NP, 8, CC), F32),
            pltpu.VMEM((2, 16, FC), jnp.int32),
            pltpu.SMEM((NP,), F32),
            tile(MROWS),
            tile(MROWS),
            pltpu.SemaphoreType.DMA((5,)),
        ],
        compiler_params=pltpu.CompilerParams(vmem_limit_bytes=8 << 20),
        cost_estimate=pl.CostEstimate(flops=20000, bytes_accessed=200000, transcendentals=0),
        name="strips",
    )(*(pltpu.with_memory_space_constraint(x, pltpu.HBM) for x in (coarse, labels, mobility)))
    rows, cols = lax.axis_size("gy"), lax.axis_size("gz")
    yb = exchanged(to_b, [((i, j), ((i + 1) % rows, j)) for i in range(1, rows, 2) for j in range(cols)])
    ya = paired(to_a, "gy", 0)
    columns = pl.pallas_call(
        columns_kernel,
        out_shape=tile(16),
        in_specs=[vmem, vmem],
        out_specs=vmem,
        compiler_params=pltpu.CompilerParams(vmem_limit_bytes=8 << 20),
        cost_estimate=pl.CostEstimate(flops=20000, bytes_accessed=200000, transcendentals=0),
        name="columns",
    )(coarse, labels)
    sides = pl.pallas_call(
        sides_kernel,
        out_shape=tile(24),
        in_specs=[vmem] * 3,
        out_specs=vmem,
        compiler_params=pltpu.CompilerParams(vmem_limit_bytes=8 << 20),
        cost_estimate=pl.CostEstimate(flops=20000, bytes_accessed=40000, transcendentals=0),
        name="sides",
    )(columns, ya, yb)
    last = cols - 2
    first_rows = (0,)
    za0 = exchanged(sides, [((i, j), (i, j + 1)) for i in range(rows) for j in range(0, cols, 2) if j < last or i in first_rows])
    zb = paired(sides, "gz", 1)
    sides, zb = lax.optimization_barrier((sides, zb))
    za1 = exchanged(sides, [((i, last), (i, last + 1)) for i in range(rows) if i not in first_rows])
    return pl.pallas_call(
        relax_kernel,
        out_shape=jax.ShapeDtypeStruct((NP, 2, FR, FC), F32),
        in_specs=[vmem] * 8,
        out_specs=hbm,
        scratch_shapes=[
            tile(NP * 48),
            tile(NP, 48),
            tile(NP, 48),
            tile(NP, 88),
            tile(NP, 88),
            tile(2, 80),
            tile(2, 80),
            tile(2, NP, 80),
            tile(2, NP, 80),
            tile(NP, 2, FR),
            pltpu.SemaphoreType.DMA((3,)),
        ],
        compiler_params=pltpu.CompilerParams(vmem_limit_bytes=16 << 20),
        cost_estimate=pl.CostEstimate(flops=8000000, bytes_accessed=900000, transcendentals=0),
        name="relax",
    )(rates, coarse, labels, ya, yb, za0, za1, zb)


def solution(mesh):
    in_specs = (P(None, None, "gy", "gz"), P(None, "gy", "gz"), P())
    out_specs = P(None, None, "gy", "gz")
    return jax.shard_map(shards, mesh=mesh, in_specs=in_specs, out_specs=out_specs, check_vma=False)
```

```python
import jax
import jax.numpy as jnp
from jax import lax
from jax.experimental import pallas as pl
from jax.experimental.pallas import tpu as pltpu
from jax.sharding import PartitionSpec as P

STEP = 0.075
NP = 8
CR, CC = 32, 64
FR, FC = 64, 128
MROWS = 16
F32 = jnp.float32


def lanes(rows):
    return lax.broadcasted_iota(jnp.int32, (rows, 128), 1)


def parities():
    return lax.axis_index("gy") % 2 == 0, lax.axis_index("gz") % 2 == 0


def strips_kernel(coarse_hbm, labels_hbm, mobility_hbm, to_a, to_b, rates, top, bottom, marks, mobility, low, high, second, sems):
    copies = [
        pltpu.make_async_copy(src, dst, sems.at[i])
        for i, (src, dst) in enumerate(
            (
                (coarse_hbm.at[:, 0:8, :], top),
                (coarse_hbm.at[:, CR - 8 : CR, :], bottom),
                (labels_hbm.at[:, 0:8, :], marks.at[:, 0:8, :]),
                (labels_hbm.at[:, FR - 8 : FR, :], marks.at[:, 8:16, :]),
                (mobility_hbm, mobility),
            )
        )
    ]
    for copy in copies:
        copy.start()
    y_even, _ = parities()
    for copy in copies:
        copy.wait()
    for row, block, strip in ((0, top, low), (6, bottom, high)):
        for p in range(NP):
            strip[p : p + 1, 0:CC] = block[p, row : row + 1, :]
            second[p : p + 1, 0:CC] = block[p, row + 1 : row + 2, :]
        strip[0:8, :] = jnp.where(lanes(8) < CC, strip[0:8, :], pltpu.roll(second[...], CC, 1))
        for x in range(2):
            strip[8 + x : 9 + x, :] = marks[x, 15 * (row // 6) : 15 * (row // 6) + 1, :].astype(F32)
        strip[10:16, :] = jnp.zeros((6, 128), F32)
    to_a[...] = jnp.where(y_even, high[...], low[...])
    to_b[...] = jnp.where(y_even, low[...], high[...])
    for p in range(NP):
        rates[p : p + 1, :] = jnp.full((1, 128), STEP * mobility[p], F32)


def write_columns(coarse, labels, sides):
    lane = lanes(8)
    first, last = jnp.zeros((8, 128), F32), jnp.zeros((8, 128), F32)
    for g in range(4):
        start = 64 * (g // 2) + 2 * (g % 2)
        for p in range(NP):
            own = jnp.concatenate([coarse[p, 8 * g : 8 * g + 8, :], jnp.zeros((8, CC), F32)], axis=1)
            at = start + 4 * p
            first = jnp.where(lane // 2 == at // 2, pltpu.roll(own, at, 1), first)
            last = jnp.where(lane // 2 == at // 2, pltpu.roll(own, (at - 62) % 128, 1), last)
        for k in range(4):
            at = start + 32 + 4 * k
            cells = labels[k % 2, 32 * (k // 2) + 8 * g : 32 * (k // 2) + 8 * g + 8, :].astype(F32)
            first = jnp.where(lane == at, pltpu.roll(cells, at, 1), first)
            last = jnp.where(lane == at, pltpu.roll(cells, at + 1, 1), last)
    sides[0:8, :] = first
    sides[8:16, :] = last


def columns_kernel(coarse, labels, sides):
    @pl.when(lax.axis_index("gy") != 0)
    def _():
        write_columns(coarse, labels, sides)


def picked(ya0, ya1, yb):
    y_even, _ = parities()
    return jnp.where(y_even, yb, ya0), jnp.where(y_even, ya1, yb)


def sides_kernel(coarse, labels, columns, ya, yb, sides):
    row = lax.axis_index("gy")

    @pl.when(row != 0)
    def _():
        sides[0:16, :] = columns[...]

    @pl.when(row == 0)
    def _():
        write_columns(coarse, labels, sides)

    lane = lanes(8)
    ends = jnp.zeros((8, 128), F32)
    for j, strip in enumerate(picked(ya[0, 0:8], ya[1, 0:8], yb[0:8])):
        for i in range(2):
            at = 64 + 16 * j + 8 * i
            ends = jnp.where(lane // 2 == at // 2, pltpu.roll(strip, (at - 62 - 64 * i) % 128, 1), ends)
            ends = jnp.where(lane // 2 == at // 2 + 1, pltpu.roll(strip, (at + 2 - 64 * i) % 128, 1), ends)
    sides[16:24, :] = ends


def z_weights():
    k = lax.broadcasted_iota(jnp.int32, (256, 256), 0) % 128
    n = lax.broadcasted_iota(jnp.int32, (256, 256), 1)
    z = jnp.where(n < 128, n, jnp.where(n == 128, -1, jnp.where(n == 255, 128, jnp.where(n == 254, -2, jnp.where(n == 253, 129, 999)))))
    column = jnp.where(k < 64, k, jnp.where(k < 66, k - 66, jnp.where(k < 68, k - 2, -999)))
    near = z >> 1
    far = near + 2 * (z & 1) - 1
    return (0.75 * (column == near).astype(F32) + 0.25 * (column == far).astype(F32)).astype(jnp.bfloat16)


def relax_kernel(rates, coarse, labels, ya, yb, za0, za1, zb, out_hbm, pad, zm, ze, fm, fe, lm, le, pm, pe, out, sems):
    _, z_even = parities()
    low, high = picked(ya[0], ya[1], yb[...])
    za = za0[...] + za1[...]
    left = jnp.where(z_even, zb[0], za)
    right = jnp.where(z_even, za, zb[1])

    lane8 = lanes(8)
    first_lane, last_lane = lane8 == 0, lane8 == 127
    west, east = left[8:16], right[0:8]
    for g in range(4):
        start = 64 * (g // 2) + 2 * (g % 2)
        for p in range(NP):
            at = start + 4 * p
            beside = jnp.where(lane8 < 66, pltpu.roll(west, (64 - at) % 128, 1), pltpu.roll(east, (66 - at) % 128, 1))
            pad[48 * p + 8 + 8 * g : 48 * p + 16 + 8 * g, :] = beside
        for k in range(4):
            rows = slice(8 + 32 * (k // 2) + 8 * g, 16 + 32 * (k // 2) + 8 * g)
            at = start + 32 + 4 * k
            le[k % 2, rows, :] = jnp.where(first_lane, pltpu.roll(west, 128 - at, 1), pltpu.roll(east, 127 - at, 1))
    for p in range(NP):
        pad[48 * p + 8 : 48 * p + 8 + CR, 0:CC] = coarse[p]
    ends = jnp.where(lane8 % 4 < 2, left[16:24], right[16:24])
    for j, strip in enumerate((low, high)):
        for i in range(2):
            beside = pltpu.roll(ends, (-16 * j - 8 * i) % 128, 1)
            cells = pltpu.roll(strip[0:8], CC, 1) if i else strip[0:8]
            pad[pl.ds(6 + 34 * j + i, NP, stride=48), :] = jnp.where(lane8 < CC, cells, beside)

    cells = pad[...]
    first = cells.astype(jnp.bfloat16)
    second = (cells - first.astype(F32)).astype(jnp.bfloat16)
    fine = jnp.dot(jnp.concatenate([first, second], axis=1), z_weights(), preferred_element_type=F32)
    zm[...] = fine[:, :128].reshape(NP, 48, 128)
    ze[...] = fine[:, 128:].reshape(NP, 48, 128)
    for p in range(NP):
        for src, dst in ((zm, fm), (ze, fe)):
            mid = 0.75 * src[p, 7:41, :]
            dst[p, pl.ds(6, 34, stride=2), :] = mid + 0.25 * src[p, 6:40, :]
            dst[p, pl.ds(7, 34, stride=2), :] = mid + 0.25 * src[p, 8:42, :]

    for x in range(2):
        lm[x, 8 : 8 + FR, :] = labels[x].astype(F32)
        lm[x, 7:8, :] = low[8 + x : 9 + x]
        lm[x, 72:73, :] = high[8 + x : 9 + x]

    rate = [rates[p : p + 1, :] for p in range(NP)]

    for t in range(9):
        here = pl.ds(7 + 8 * t, 8)
        above, below = pl.ds(6 + 8 * t, 8), pl.ds(8 + 8 * t, 8)
        ms = [fm[p, here, :] for p in range(NP)]
        es = [fe[p, here, :] for p in range(NP)]
        sm = 4.0 + sum(m * m for m in ms)
        se = 4.0 + sum(e * e for e in es)
        marks_m = [lm[x, here, :] for x in range(2)]
        marks_e = [le[x, here, :] for x in range(2)]
        for p in range(NP):
            m, e = fm[p, here, :], fe[p, here, :]
            west = jnp.where(first_lane, e, pltpu.roll(m, 1, 1))
            east = jnp.where(last_lane, e, pltpu.roll(m, 127, 1))
            lap = (fm[p, above, :] + fm[p, below, :]) + (west + east)
            base = m + rate[p] * (lap - sm * m)
            lap_e = (fe[p, above, :] + fe[p, below, :]) + (m + pltpu.roll(e, 2, 1))
            base_e = e + rate[p] * (lap_e - se * e)
            for x in range(2):
                pm[x, p, here, :] = jnp.where(marks_m[x] == p, base + rate[p], base)
                pe[x, p, here, :] = jnp.where(marks_e[x] == p, base_e + rate[p], base_e)

    copies = []
    for t in range(8):
        here = pl.ds(8 + 8 * t, 8)
        above, below = pl.ds(7 + 8 * t, 8), pl.ds(9 + 8 * t, 8)
        for x in range(2):
            ms = [pm[x, p, here, :] for p in range(NP)]
            sm = 6.0 + sum(m * m for m in ms)
            marks_m = lm[x, here, :]
            for p in range(NP):
                m, e, other = ms[p], pe[x, p, here, :], pm[1 - x, p, here, :]
                west = jnp.where(first_lane, e, pltpu.roll(m, 1, 1))
                east = jnp.where(last_lane, e, pltpu.roll(m, 127, 1))
                lap = (pm[x, p, above, :] + pm[x, p, below, :]) + (west + east) + (other + other)
                change = lap - sm * m
                change = jnp.where(marks_m == p, change + 1.0, change)
                out[p, x, 8 * t : 8 * t + 8, :] = m + rate[p] * change
        if t in (2, 5, 7):
            part = (2, 5, 7).index(t)
            rows = pl.ds(24 * part, 24 if t < 7 else 16)
            copies.append(pltpu.make_async_copy(out.at[:, :, rows, :], out_hbm.at[:, :, rows, :], sems.at[part]))
            copies[-1].start()
    for copy in copies:
        copy.wait()


def exchanged(cells, pairs):
    width = lax.axis_size("gz")
    flat = [(i * width + j, k * width + l) for (i, j), (k, l) in pairs]
    return lax.ppermute(cells, ("gy", "gz"), flat + [(b, a) for a, b in flat])


def paired(cells, axis, odd):
    count = lax.axis_size(axis)
    return lax.all_gather(cells, axis, axis_index_groups=[[i, (i + 1) % count] for i in range(odd, count, 2)])


def shards(coarse, labels, mobility):
    coarse = coarse.reshape(NP, CR, CC)
    vmem = pl.BlockSpec(memory_space=pltpu.VMEM)
    hbm = pl.BlockSpec(memory_space=pltpu.HBM)
    tile = lambda *shape: pltpu.VMEM(shape + (128,), F32)
    to_a, to_b, rates = pl.pallas_call(
        strips_kernel,
        out_shape=(tile(MROWS), tile(MROWS), tile(8)),
        in_specs=[hbm, hbm, hbm],
        out_specs=(vmem,) * 3,
        scratch_shapes=[
            pltpu.VMEM((NP, 8, CC), F32),
            pltpu.VMEM((NP, 8, CC), F32),
            pltpu.VMEM((2, 16, FC), jnp.int32),
            pltpu.SMEM((NP,), F32),
            tile(MROWS),
            tile(MROWS),
            tile(8),
            pltpu.SemaphoreType.DMA((5,)),
        ],
        compiler_params=pltpu.CompilerParams(vmem_limit_bytes=8 << 20),
        cost_estimate=pl.CostEstimate(flops=20000, bytes_accessed=200000, transcendentals=0),
        name="strips",
    )(*(pltpu.with_memory_space_constraint(x, pltpu.HBM) for x in (coarse, labels, mobility)))
    rows, cols = lax.axis_size("gy"), lax.axis_size("gz")
    yb = exchanged(to_b, [((i, j), ((i + 1) % rows, j)) for i in range(1, rows, 2) for j in range(cols)])
    ya = paired(to_a, "gy", 0)
    columns = pl.pallas_call(
        columns_kernel,
        out_shape=tile(16),
        in_specs=[vmem, vmem],
        out_specs=vmem,
        compiler_params=pltpu.CompilerParams(vmem_limit_bytes=8 << 20),
        cost_estimate=pl.CostEstimate(flops=20000, bytes_accessed=200000, transcendentals=0),
        name="columns",
    )(coarse, labels)
    sides = pl.pallas_call(
        sides_kernel,
        out_shape=tile(24),
        in_specs=[vmem] * 5,
        out_specs=vmem,
        compiler_params=pltpu.CompilerParams(vmem_limit_bytes=8 << 20),
        cost_estimate=pl.CostEstimate(flops=20000, bytes_accessed=40000, transcendentals=0),
        name="sides",
    )(coarse, labels, columns, ya, yb)
    last = cols - 2
    first_rows = (0,)
    za0 = exchanged(sides, [((i, j), (i, j + 1)) for i in range(rows) for j in range(0, cols, 2) if j < last or i in first_rows])
    zb = paired(sides, "gz", 1)
    sides, zb = lax.optimization_barrier((sides, zb))
    za1 = exchanged(sides, [((i, last), (i, last + 1)) for i in range(rows) if i not in first_rows])
    return pl.pallas_call(
        relax_kernel,
        out_shape=jax.ShapeDtypeStruct((NP, 2, FR, FC), F32),
        in_specs=[vmem] * 8,
        out_specs=hbm,
        scratch_shapes=[
            tile(NP * 48),
            tile(NP, 48),
            tile(NP, 48),
            tile(NP, 88),
            tile(NP, 88),
            tile(2, 80),
            tile(2, 80),
            tile(2, NP, 80),
            tile(2, NP, 80),
            tile(NP, 2, FR),
            pltpu.SemaphoreType.DMA((3,)),
        ],
        compiler_params=pltpu.CompilerParams(vmem_limit_bytes=16 << 20),
        cost_estimate=pl.CostEstimate(flops=8000000, bytes_accessed=900000, transcendentals=0),
        name="relax",
    )(rates, coarse, labels, ya, yb, za0, za1, zb)


def solution(mesh):
    in_specs = (P(None, None, "gy", "gz"), P(None, "gy", "gz"), P())
    out_specs = P(None, None, "gy", "gz")
    return jax.shard_map(shards, mesh=mesh, in_specs=in_specs, out_specs=out_specs, check_vma=False)
```

```python
import jax
import jax.numpy as jnp
from jax import lax
from jax.experimental import pallas as pl
from jax.experimental.pallas import tpu as pltpu
from jax.sharding import PartitionSpec as P

STEP = 0.075
NP = 8
CR, CC = 32, 64
FR, FC = 64, 128
MROWS = 16
F32 = jnp.float32


def lanes(rows):
    return lax.broadcasted_iota(jnp.int32, (rows, 128), 1)


def parities():
    return lax.axis_index("gy") % 2 == 0, lax.axis_index("gz") % 2 == 0


def strips_kernel(coarse_hbm, labels_hbm, mobility_hbm, to_a, to_b, rates, top, bottom, marks, mobility, low, high, sems):
    copies = [
        pltpu.make_async_copy(src, dst, sems.at[i])
        for i, (src, dst) in enumerate(
            (
                (coarse_hbm.at[:, 0:8, :], top),
                (coarse_hbm.at[:, CR - 8 : CR, :], bottom),
                (labels_hbm.at[:, 0:8, :], marks.at[:, 0:8, :]),
                (labels_hbm.at[:, FR - 8 : FR, :], marks.at[:, 8:16, :]),
                (mobility_hbm, mobility),
            )
        )
    ]
    for copy in copies:
        copy.start()
    y_even, _ = parities()
    for copy in copies:
        copy.wait()
    for row, block, strip in ((0, top, low), (6, bottom, high)):
        for p in range(NP):
            strip[p : p + 1, 0:CC] = block[p, row : row + 1, :]
            strip[p : p + 1, CC : 2 * CC] = block[p, row + 1 : row + 2, :]
        for x in range(2):
            strip[8 + x : 9 + x, :] = marks[x, 15 * (row // 6) : 15 * (row // 6) + 1, :].astype(F32)
        strip[10:16, :] = jnp.zeros((6, 128), F32)
    to_a[...] = jnp.where(y_even, high[...], low[...])
    to_b[...] = jnp.where(y_even, low[...], high[...])
    for p in range(NP):
        rates[p : p + 1, :] = jnp.full((1, 128), STEP * mobility[p], F32)


def columns_kernel(coarse, labels, sides):
    lane = lanes(8)
    first, last = jnp.zeros((8, 128), F32), jnp.zeros((8, 128), F32)
    for g in range(4):
        start = 64 * (g // 2) + 2 * (g % 2)
        for p in range(NP):
            own = jnp.concatenate([coarse[p, 8 * g : 8 * g + 8, :], jnp.zeros((8, CC), F32)], axis=1)
            at = start + 4 * p
            first = jnp.where(lane // 2 == at // 2, pltpu.roll(own, at, 1), first)
            last = jnp.where(lane // 2 == at // 2, pltpu.roll(own, (at - 62) % 128, 1), last)
        for k in range(4):
            at = start + 32 + 4 * k
            cells = labels[k % 2, 32 * (k // 2) + 8 * g : 32 * (k // 2) + 8 * g + 8, :].astype(F32)
            first = jnp.where(lane == at, pltpu.roll(cells, at, 1), first)
            last = jnp.where(lane == at, pltpu.roll(cells, at + 1, 1), last)
    sides[0:8, :] = first
    sides[8:16, :] = last


def picked(ya0, ya1, yb):
    y_even, _ = parities()
    return jnp.where(y_even, yb, ya0), jnp.where(y_even, ya1, yb)


def sides_kernel(columns, ya, yb, sides):
    lane = lanes(8)
    first, last = columns[0:8, :], columns[8:16, :]
    for j, strip in enumerate(picked(ya[0, 0:8], ya[1, 0:8], yb[0:8])):
        for i in range(2):
            at = 50 + 4 * j + 2 * i
            first = jnp.where(lane // 2 == at // 2, pltpu.roll(strip, (at - 64 * i) % 128, 1), first)
            last = jnp.where(lane // 2 == at // 2, pltpu.roll(strip, (at - 62 - 64 * i) % 128, 1), last)
    sides[0:8, :] = first
    sides[8:16, :] = last


def z_weights():
    k = lax.broadcasted_iota(jnp.int32, (256, 256), 0) % 128
    n = lax.broadcasted_iota(jnp.int32, (256, 256), 1)
    z = jnp.where(n < 128, n, jnp.where(n == 128, -1, jnp.where(n == 255, 128, jnp.where(n == 254, -2, jnp.where(n == 253, 129, 999)))))
    column = jnp.where(k < 64, k, jnp.where(k < 66, k - 66, jnp.where(k < 68, k - 2, -999)))
    near = z >> 1
    far = near + 2 * (z & 1) - 1
    return (0.75 * (column == near).astype(F32) + 0.25 * (column == far).astype(F32)).astype(jnp.bfloat16)


def relax_kernel(rates, coarse, labels, ya, yb, za0, za1, zb, out_hbm, pad, zm, ze, fm, fe, lm, le, pm, pe, out, sems):
    _, z_even = parities()
    low, high = picked(ya[0], ya[1], yb[...])
    za = za0[...] + za1[...]
    left = jnp.where(z_even, zb[0], za)
    right = jnp.where(z_even, za, zb[1])

    lane8 = lanes(8)
    first_lane, last_lane = lane8 == 0, lane8 == 127
    west, east = left[8:16], right[0:8]
    for g in range(4):
        start = 64 * (g // 2) + 2 * (g % 2)
        for p in range(NP):
            at = start + 4 * p
            beside = jnp.where(lane8 < 66, pltpu.roll(west, (64 - at) % 128, 1), pltpu.roll(east, (66 - at) % 128, 1))
            pad[48 * p + 8 + 8 * g : 48 * p + 16 + 8 * g, :] = beside
        for k in range(4):
            rows = slice(8 + 32 * (k // 2) + 8 * g, 16 + 32 * (k // 2) + 8 * g)
            at = start + 32 + 4 * k
            le[k % 2, rows, :] = jnp.where(first_lane, pltpu.roll(west, 128 - at, 1), pltpu.roll(east, 127 - at, 1))
    for p in range(NP):
        pad[48 * p + 8 : 48 * p + 8 + CR, 0:CC] = coarse[p]
    for j, strip in enumerate((low, high)):
        for i in range(2):
            at = 50 + 4 * j + 2 * i
            beside = jnp.where(lane8 < 66, pltpu.roll(west, 64 - at, 1), pltpu.roll(east, 66 - at, 1))
            cells = pltpu.roll(strip[0:8], CC, 1) if i else strip[0:8]
            pad[pl.ds(6 + 34 * j + i, NP, stride=48), :] = jnp.where(lane8 < CC, cells, beside)

    cells = pad[...]
    first = cells.astype(jnp.bfloat16)
    second = (cells - first.astype(F32)).astype(jnp.bfloat16)
    fine = jnp.dot(jnp.concatenate([first, second], axis=1), z_weights(), preferred_element_type=F32)
    zm[...] = fine[:, :128].reshape(NP, 48, 128)
    ze[...] = fine[:, 128:].reshape(NP, 48, 128)
    for p in range(NP):
        for src, dst in ((zm, fm), (ze, fe)):
            mid = 0.75 * src[p, 7:41, :]
            dst[p, pl.ds(6, 34, stride=2), :] = mid + 0.25 * src[p, 6:40, :]
            dst[p, pl.ds(7, 34, stride=2), :] = mid + 0.25 * src[p, 8:42, :]

    for x in range(2):
        lm[x, 8 : 8 + FR, :] = labels[x].astype(F32)
        lm[x, 7:8, :] = low[8 + x : 9 + x]
        lm[x, 72:73, :] = high[8 + x : 9 + x]

    rate = [rates[p : p + 1, :] for p in range(NP)]

    for t in range(9):
        here = pl.ds(7 + 8 * t, 8)
        above, below = pl.ds(6 + 8 * t, 8), pl.ds(8 + 8 * t, 8)
        ms = [fm[p, here, :] for p in range(NP)]
        es = [fe[p, here, :] for p in range(NP)]
        sm = 4.0 + sum(m * m for m in ms)
        se = 4.0 + sum(e * e for e in es)
        marks_m = [lm[x, here, :] for x in range(2)]
        marks_e = [le[x, here, :] for x in range(2)]
        for p in range(NP):
            m, e = ms[p], es[p]
            west = jnp.where(first_lane, e, pltpu.roll(m, 1, 1))
            east = jnp.where(last_lane, e, pltpu.roll(m, 127, 1))
            lap = (fm[p, above, :] + fm[p, below, :]) + (west + east)
            base = m + rate[p] * (lap - sm * m)
            lap_e = (fe[p, above, :] + fe[p, below, :]) + (m + pltpu.roll(e, 2, 1))
            base_e = e + rate[p] * (lap_e - se * e)
            for x in range(2):
                pm[x, p, here, :] = jnp.where(marks_m[x] == p, base + rate[p], base)
                pe[x, p, here, :] = jnp.where(marks_e[x] == p, base_e + rate[p], base_e)

    copies = []
    for t in range(8):
        here = pl.ds(8 + 8 * t, 8)
        above, below = pl.ds(7 + 8 * t, 8), pl.ds(9 + 8 * t, 8)
        for x in range(2):
            ms = [pm[x, p, here, :] for p in range(NP)]
            sm = 6.0 + sum(m * m for m in ms)
            marks_m = lm[x, here, :]
            for p in range(NP):
                m, e, other = ms[p], pe[x, p, here, :], pm[1 - x, p, here, :]
                west = jnp.where(first_lane, e, pltpu.roll(m, 1, 1))
                east = jnp.where(last_lane, e, pltpu.roll(m, 127, 1))
                lap = (pm[x, p, above, :] + pm[x, p, below, :]) + (west + east) + (other + other)
                change = lap - sm * m
                change = jnp.where(marks_m == p, change + 1.0, change)
                out[p, x, 8 * t : 8 * t + 8, :] = m + rate[p] * change
        if t in (2, 5, 7):
            part = (2, 5, 7).index(t)
            rows = pl.ds(24 * part, 24 if t < 7 else 16)
            copies.append(pltpu.make_async_copy(out.at[:, :, rows, :], out_hbm.at[:, :, rows, :], sems.at[part]))
            copies[-1].start()
    for copy in copies:
        copy.wait()


def exchanged(cells, pairs):
    width = lax.axis_size("gz")
    flat = [(i * width + j, k * width + l) for (i, j), (k, l) in pairs]
    return lax.ppermute(cells, ("gy", "gz"), flat + [(b, a) for a, b in flat])


def paired(cells, axis, odd):
    count = lax.axis_size(axis)
    return lax.all_gather(cells, axis, axis_index_groups=[[i, (i + 1) % count] for i in range(odd, count, 2)])


def shards(coarse, labels, mobility):
    coarse = coarse.reshape(NP, CR, CC)
    vmem = pl.BlockSpec(memory_space=pltpu.VMEM)
    hbm = pl.BlockSpec(memory_space=pltpu.HBM)
    tile = lambda *shape: pltpu.VMEM(shape + (128,), F32)
    to_a, to_b, rates = pl.pallas_call(
        strips_kernel,
        out_shape=(tile(MROWS), tile(MROWS), tile(8)),
        in_specs=[hbm, hbm, hbm],
        out_specs=(vmem,) * 3,
        scratch_shapes=[
            pltpu.VMEM((NP, 8, CC), F32),
            pltpu.VMEM((NP, 8, CC), F32),
            pltpu.VMEM((2, 16, FC), jnp.int32),
            pltpu.SMEM((NP,), F32),
            tile(MROWS),
            tile(MROWS),
            pltpu.SemaphoreType.DMA((5,)),
        ],
        compiler_params=pltpu.CompilerParams(vmem_limit_bytes=8 << 20),
        cost_estimate=pl.CostEstimate(flops=20000, bytes_accessed=200000, transcendentals=0),
        name="strips",
    )(*(pltpu.with_memory_space_constraint(x, pltpu.HBM) for x in (coarse, labels, mobility)))
    rows, cols = lax.axis_size("gy"), lax.axis_size("gz")
    yb = exchanged(to_b, [((i, j), ((i + 1) % rows, j)) for i in range(1, rows, 2) for j in range(cols)])
    ya = paired(to_a, "gy", 0)
    columns = pl.pallas_call(
        columns_kernel,
        out_shape=tile(16),
        in_specs=[vmem, vmem],
        out_specs=vmem,
        compiler_params=pltpu.CompilerParams(vmem_limit_bytes=8 << 20),
        cost_estimate=pl.CostEstimate(flops=20000, bytes_accessed=200000, transcendentals=0),
        name="columns",
    )(coarse, labels)
    sides = pl.pallas_call(
        sides_kernel,
        out_shape=tile(MROWS),
        in_specs=[vmem] * 3,
        out_specs=vmem,
        compiler_params=pltpu.CompilerParams(vmem_limit_bytes=8 << 20),
        cost_estimate=pl.CostEstimate(flops=20000, bytes_accessed=40000, transcendentals=0),
        name="sides",
    )(columns, ya, yb)
    last = cols - 2
    first_rows = (0,)
    za0 = exchanged(sides, [((i, j), (i, j + 1)) for i in range(rows) for j in range(0, cols, 2) if j < last or i in first_rows])
    zb = paired(sides, "gz", 1)
    sides, zb, za0 = lax.optimization_barrier((sides, zb, za0))
    za1 = exchanged(sides, [((i, last), (i, last + 1)) for i in range(rows) if i not in first_rows])
    return pl.pallas_call(
        relax_kernel,
        out_shape=jax.ShapeDtypeStruct((NP, 2, FR, FC), F32),
        in_specs=[vmem] * 8,
        out_specs=hbm,
        scratch_shapes=[
            tile(NP * 48),
            tile(NP, 48),
            tile(NP, 48),
            tile(NP, 88),
            tile(NP, 88),
            tile(2, 80),
            tile(2, 80),
            tile(2, NP, 80),
            tile(2, NP, 80),
            tile(NP, 2, FR),
            pltpu.SemaphoreType.DMA((3,)),
        ],
        compiler_params=pltpu.CompilerParams(vmem_limit_bytes=16 << 20),
        cost_estimate=pl.CostEstimate(flops=8000000, bytes_accessed=900000, transcendentals=0),
        name="relax",
    )(rates, coarse, labels, ya, yb, za0, za1, zb)


def solution(mesh):
    in_specs = (P(None, None, "gy", "gz"), P(None, "gy", "gz"), P())
    out_specs = P(None, None, "gy", "gz")
    return jax.shard_map(shards, mesh=mesh, in_specs=in_specs, out_specs=out_specs, check_vma=False)
```

```python
import jax
import jax.numpy as jnp
from jax import lax
from jax.experimental import pallas as pl
from jax.experimental.pallas import tpu as pltpu
from jax.sharding import PartitionSpec as P

STEP = 0.075
NP = 8
CR, CC = 32, 64
FR, FC = 64, 128
MROWS = 16
F32 = jnp.float32


def lanes(rows):
    return lax.broadcasted_iota(jnp.int32, (rows, 128), 1)


def parities():
    return lax.axis_index("gy") % 2 == 0, lax.axis_index("gz") % 2 == 0


def strips_kernel(coarse_hbm, labels_hbm, mobility_hbm, to_a, to_b, rates, top, bottom, marks, mobility, low, high, second, sems):
    copies = [
        pltpu.make_async_copy(src, dst, sems.at[i])
        for i, (src, dst) in enumerate(
            (
                (coarse_hbm.at[:, 0:8, :], top),
                (coarse_hbm.at[:, CR - 8 : CR, :], bottom),
                (labels_hbm.at[:, 0:8, :], marks.at[:, 0:8, :]),
                (labels_hbm.at[:, FR - 8 : FR, :], marks.at[:, 8:16, :]),
                (mobility_hbm, mobility),
            )
        )
    ]
    for copy in copies:
        copy.start()
    y_even, _ = parities()
    for copy in copies:
        copy.wait()
    for row, block, strip in ((0, top, low), (6, bottom, high)):
        for p in range(NP):
            strip[p : p + 1, 0:CC] = block[p, row : row + 1, :]
            second[p : p + 1, 0:CC] = block[p, row + 1 : row + 2, :]
        strip[0:8, :] = jnp.where(lanes(8) < CC, strip[0:8, :], pltpu.roll(second[...], CC, 1))
        for x in range(2):
            strip[8 + x : 9 + x, :] = marks[x, 15 * (row // 6) : 15 * (row // 6) + 1, :].astype(F32)
        strip[10:16, :] = jnp.zeros((6, 128), F32)
    to_a[...] = jnp.where(y_even, high[...], low[...])
    to_b[...] = jnp.where(y_even, low[...], high[...])
    for p in range(NP):
        rates[p : p + 1, :] = jnp.full((1, 128), STEP * mobility[p], F32)


def columns_kernel(coarse, labels, sides):
    lane = lanes(8)
    first, last = jnp.zeros((8, 128), F32), jnp.zeros((8, 128), F32)
    for g in range(4):
        start = 64 * (g // 2) + 2 * (g % 2)
        for p in range(NP):
            own = jnp.concatenate([coarse[p, 8 * g : 8 * g + 8, :], jnp.zeros((8, CC), F32)], axis=1)
            at = start + 4 * p
            first = jnp.where(lane // 2 == at // 2, pltpu.roll(own, at, 1), first)
            last = jnp.where(lane // 2 == at // 2, pltpu.roll(own, (at - 62) % 128, 1), last)
        for k in range(4):
            at = start + 32 + 4 * k
            cells = labels[k % 2, 32 * (k // 2) + 8 * g : 32 * (k // 2) + 8 * g + 8, :].astype(F32)
            first = jnp.where(lane == at, pltpu.roll(cells, at, 1), first)
            last = jnp.where(lane == at, pltpu.roll(cells, at + 1, 1), last)
    sides[0:8, :] = first
    sides[8:16, :] = last


def picked(ya0, ya1, yb):
    y_even, _ = parities()
    return jnp.where(y_even, yb, ya0), jnp.where(y_even, ya1, yb)


def sides_kernel(columns, ya, yb, sides):
    lane = lanes(8)
    first, last = columns[0:8, :], columns[8:16, :]
    for j, strip in enumerate(picked(ya[0, 0:8], ya[1, 0:8], yb[0:8])):
        for i in range(2):
            at = 50 + 4 * j + 2 * i
            first = jnp.where(lane // 2 == at // 2, pltpu.roll(strip, (at - 64 * i) % 128, 1), first)
            last = jnp.where(lane // 2 == at // 2, pltpu.roll(strip, (at - 62 - 64 * i) % 128, 1), last)
    sides[0:8, :] = first
    sides[8:16, :] = last


def z_weights():
    k = lax.broadcasted_iota(jnp.int32, (256, 256), 0) % 128
    n = lax.broadcasted_iota(jnp.int32, (256, 256), 1)
    z = jnp.where(n < 128, n, jnp.where(n == 128, -1, jnp.where(n == 255, 128, jnp.where(n == 254, -2, jnp.where(n == 253, 129, 999)))))
    column = jnp.where(k < 64, k, jnp.where(k < 66, k - 66, jnp.where(k < 68, k - 2, -999)))
    near = z >> 1
    far = near + 2 * (z & 1) - 1
    return (0.75 * (column == near).astype(F32) + 0.25 * (column == far).astype(F32)).astype(jnp.bfloat16)


def relax_kernel(rates, coarse, labels, ya, yb, za0, za1, zb, out_hbm, pad, zm, ze, fm, fe, lm, le, pm, pe, out, sems):
    _, z_even = parities()
    low, high = picked(ya[0], ya[1], yb[...])
    za = za0[...] + za1[...]
    left = jnp.where(z_even, zb[0], za)
    right = jnp.where(z_even, za, zb[1])

    lane8 = lanes(8)
    first_lane, last_lane = lane8 == 0, lane8 == 127
    west, east = left[8:16], right[0:8]
    for g in range(4):
        start = 64 * (g // 2) + 2 * (g % 2)
        for p in range(NP):
            at = start + 4 * p
            beside = jnp.where(lane8 < 66, pltpu.roll(west, (64 - at) % 128, 1), pltpu.roll(east, (66 - at) % 128, 1))
            pad[48 * p + 8 + 8 * g : 48 * p + 16 + 8 * g, :] = beside
        for k in range(4):
            rows = slice(8 + 32 * (k // 2) + 8 * g, 16 + 32 * (k // 2) + 8 * g)
            at = start + 32 + 4 * k
            le[k % 2, rows, :] = jnp.where(first_lane, pltpu.roll(west, 128 - at, 1), pltpu.roll(east, 127 - at, 1))
    for p in range(NP):
        pad[48 * p + 8 : 48 * p + 8 + CR, 0:CC] = coarse[p]
    for j, strip in enumerate((low, high)):
        for i in range(2):
            at = 50 + 4 * j + 2 * i
            beside = jnp.where(lane8 < 66, pltpu.roll(west, 64 - at, 1), pltpu.roll(east, 66 - at, 1))
            cells = pltpu.roll(strip[0:8], CC, 1) if i else strip[0:8]
            pad[pl.ds(6 + 34 * j + i, NP, stride=48), :] = jnp.where(lane8 < CC, cells, beside)

    cells = pad[...]
    first = cells.astype(jnp.bfloat16)
    second = (cells - first.astype(F32)).astype(jnp.bfloat16)
    fine = jnp.dot(jnp.concatenate([first, second], axis=1), z_weights(), preferred_element_type=F32)
    zm[...] = fine[:, :128].reshape(NP, 48, 128)
    ze[...] = fine[:, 128:].reshape(NP, 48, 128)
    for p in range(NP):
        for src, dst in ((zm, fm), (ze, fe)):
            mid = 0.75 * src[p, 7:41, :]
            dst[p, pl.ds(6, 34, stride=2), :] = mid + 0.25 * src[p, 6:40, :]
            dst[p, pl.ds(7, 34, stride=2), :] = mid + 0.25 * src[p, 8:42, :]

    for x in range(2):
        lm[x, 8 : 8 + FR, :] = labels[x].astype(F32)
        lm[x, 7:8, :] = low[8 + x : 9 + x]
        lm[x, 72:73, :] = high[8 + x : 9 + x]

    rate = [rates[p : p + 1, :] for p in range(NP)]

    for t in range(9):
        here = pl.ds(7 + 8 * t, 8)
        above, below = pl.ds(6 + 8 * t, 8), pl.ds(8 + 8 * t, 8)
        ms = [fm[p, here, :] for p in range(NP)]
        es = [fe[p, here, :] for p in range(NP)]
        sm = 4.0 + sum(m * m for m in ms)
        se = 4.0 + sum(e * e for e in es)
        marks_m = [lm[x, here, :] for x in range(2)]
        marks_e = [le[x, here, :] for x in range(2)]
        for p in range(NP):
            m, e = fm[p, here, :], fe[p, here, :]
            west = jnp.where(first_lane, e, pltpu.roll(m, 1, 1))
            east = jnp.where(last_lane, e, pltpu.roll(m, 127, 1))
            lap = (fm[p, above, :] + fm[p, below, :]) + (west + east)
            base = m + rate[p] * (lap - sm * m)
            lap_e = (fe[p, above, :] + fe[p, below, :]) + (m + pltpu.roll(e, 2, 1))
            base_e = e + rate[p] * (lap_e - se * e)
            for x in range(2):
                pm[x, p, here, :] = jnp.where(marks_m[x] == p, base + rate[p], base)
                pe[x, p, here, :] = jnp.where(marks_e[x] == p, base_e + rate[p], base_e)

    copies = []
    for t in range(8):
        here = pl.ds(8 + 8 * t, 8)
        above, below = pl.ds(7 + 8 * t, 8), pl.ds(9 + 8 * t, 8)
        for x in range(2):
            ms = [pm[x, p, here, :] for p in range(NP)]
            sm = 6.0 + sum(m * m for m in ms)
            marks_m = lm[x, here, :]
            for p in range(NP):
                m, e, other = ms[p], pe[x, p, here, :], pm[1 - x, p, here, :]
                west = jnp.where(first_lane, e, pltpu.roll(m, 1, 1))
                east = jnp.where(last_lane, e, pltpu.roll(m, 127, 1))
                lap = (pm[x, p, above, :] + pm[x, p, below, :]) + (west + east) + (other + other)
                change = lap - sm * m
                change = jnp.where(marks_m == p, change + 1.0, change)
                out[p, x, 8 * t : 8 * t + 8, :] = m + rate[p] * change
        if t in (2, 5, 7):
            part = (2, 5, 7).index(t)
            rows = pl.ds(24 * part, 24 if t < 7 else 16)
            copies.append(pltpu.make_async_copy(out.at[:, :, rows, :], out_hbm.at[:, :, rows, :], sems.at[part]))
            copies[-1].start()
    for copy in copies:
        copy.wait()


def exchanged(cells, pairs):
    width = lax.axis_size("gz")
    flat = [(i * width + j, k * width + l) for (i, j), (k, l) in pairs]
    return lax.ppermute(cells, ("gy", "gz"), flat + [(b, a) for a, b in flat])


def paired(cells, axis, odd):
    count = lax.axis_size(axis)
    return lax.all_gather(cells, axis, axis_index_groups=[[i, (i + 1) % count] for i in range(odd, count, 2)])


def shards(coarse, labels, mobility):
    coarse = coarse.reshape(NP, CR, CC)
    vmem = pl.BlockSpec(memory_space=pltpu.VMEM)
    hbm = pl.BlockSpec(memory_space=pltpu.HBM)
    tile = lambda *shape: pltpu.VMEM(shape + (128,), F32)
    to_a, to_b, rates = pl.pallas_call(
        strips_kernel,
        out_shape=(tile(MROWS), tile(MROWS), tile(8)),
        in_specs=[hbm, hbm, hbm],
        out_specs=(vmem,) * 3,
        scratch_shapes=[
            pltpu.VMEM((NP, 8, CC), F32),
            pltpu.VMEM((NP, 8, CC), F32),
            pltpu.VMEM((2, 16, FC), jnp.int32),
            pltpu.SMEM((NP,), F32),
            tile(MROWS),
            tile(MROWS),
            tile(8),
            pltpu.SemaphoreType.DMA((5,)),
        ],
        compiler_params=pltpu.CompilerParams(vmem_limit_bytes=8 << 20),
        cost_estimate=pl.CostEstimate(flops=20000, bytes_accessed=200000, transcendentals=0),
        name="strips",
    )(*(pltpu.with_memory_space_constraint(x, pltpu.HBM) for x in (coarse, labels, mobility)))
    rows, cols = lax.axis_size("gy"), lax.axis_size("gz")
    yb = exchanged(to_b, [((i, j), ((i + 1) % rows, j)) for i in range(1, rows, 2) for j in range(cols)])
    ya = paired(to_a, "gy", 0)
    columns = pl.pallas_call(
        columns_kernel,
        out_shape=tile(16),
        in_specs=[vmem, vmem],
        out_specs=vmem,
        compiler_params=pltpu.CompilerParams(vmem_limit_bytes=8 << 20),
        cost_estimate=pl.CostEstimate(flops=20000, bytes_accessed=200000, transcendentals=0),
        name="columns",
    )(coarse, labels)
    sides = pl.pallas_call(
        sides_kernel,
        out_shape=tile(MROWS),
        in_specs=[vmem] * 3,
        out_specs=vmem,
        compiler_params=pltpu.CompilerParams(vmem_limit_bytes=8 << 20),
        cost_estimate=pl.CostEstimate(flops=20000, bytes_accessed=40000, transcendentals=0),
        name="sides",
    )(columns, ya, yb)
    last = cols - 2
    first_rows = (0,)
    za0 = exchanged(sides, [((i, j), (i, j + 1)) for i in range(rows) for j in range(0, cols, 2) if j < last or i in first_rows])
    zb = paired(sides, "gz", 1)
    sides, zb, za0 = lax.optimization_barrier((sides, zb, za0))
    za1 = exchanged(sides, [((i, last), (i, last + 1)) for i in range(rows) if i not in first_rows])
    return pl.pallas_call(
        relax_kernel,
        out_shape=jax.ShapeDtypeStruct((NP, 2, FR, FC), F32),
        in_specs=[vmem] * 8,
        out_specs=hbm,
        scratch_shapes=[
            tile(NP * 48),
            tile(NP, 48),
            tile(NP, 48),
            tile(NP, 88),
            tile(NP, 88),
            tile(2, 80),
            tile(2, 80),
            tile(2, NP, 80),
            tile(2, NP, 80),
            tile(NP, 2, FR),
            pltpu.SemaphoreType.DMA((3,)),
        ],
        compiler_params=pltpu.CompilerParams(vmem_limit_bytes=16 << 20),
        cost_estimate=pl.CostEstimate(flops=8000000, bytes_accessed=900000, transcendentals=0),
        name="relax",
    )(rates, coarse, labels, ya, yb, za0, za1, zb)


def solution(mesh):
    in_specs = (P(None, None, "gy", "gz"), P(None, "gy", "gz"), P())
    out_specs = P(None, None, "gy", "gz")
    return jax.shard_map(shards, mesh=mesh, in_specs=in_specs, out_specs=out_specs, check_vma=False)
```
